32 devices in a mesh: ctx: 8 (over z, x), tp: 4 (over y, core).
Axes of the slice: x: 2, y: 2, z: 4, core: 2. Of those that a mesh axis runs over, the one named last changes fastest.
Arguments:
- x_resid: bfloat16 [1024, 7168], P('ctx', 'tp'), may hold values from -4.5 to 4.5
- query_nope: bfloat16 [1024, 8192], P('ctx', 'tp'), may hold values from -6 to 6
- query_rope: bfloat16 [1024, 4096], P('ctx', 'tp'), may hold values from -8 to 8
- latent_kv: bfloat16 [512, 1024], P(None, 'ctx'), may hold values from -6 to 6
- key_rope: bfloat16 [64, 1024], P(None, 'ctx'), may hold values from -8 to 8
- absorb_key: bfloat16 [64, 128, 512], P('tp'), may hold values from -0.5 to 0.5
- absorb_value: bfloat16 [64, 512, 128], P('tp'), may hold values from -0.25 to 0.25
- out_proj: bfloat16 [8192, 7168], P('tp'), may hold values from -0.0625 to 0.0625
- norm_gain: bfloat16 [7168], replicated, may hold values from 0.099609375 to 1.8984375
- router: bfloat16 [8, 7168], replicated, may hold values from -0.0625 to 0.0625
- routes: int32 [1024, 4], P('ctx'), may hold values from 0 to 7, all different within a row; in each aligned block of 128 rows (0 to 127, 128 to 255, ...) at most 128 rows name the same one
- gate_proj: bfloat16 [8, 7168, 1024], P('ctx', None, 'tp'), may hold values from -0.0625 to 0.0625
- up_proj: bfloat16 [8, 7168, 1024], P('ctx', None, 'tp'), may hold values from -0.0625 to 0.0625
- down_proj: bfloat16 [8, 1024, 7168], P('ctx', 'tp'), may hold values from -0.1875 to 0.1875
Outputs:
- layer_out: bfloat16 [1024, 7168], P('ctx', 'tp')
The draws below stay inside these ranges and needn't reach their ends.
Inputs may be any that keep to these rules, and one draw needn't show every extreme that they name: `routes`: each row names 4 different experts; within the rows of one index of ctx no expert is named by more than 128 rows, and that many is reached.
All inputs are finite; a program needn't handle non-finite values.
Results may differ from the reference program's by a relative error of at most 0.033.
Values may be sent and summed in bfloat16 or wider, within the bound.
A program may use at most 192 MiB of HBM per device.

```python
import math
import jax
import jax.numpy as jnp
import numpy as np
from jax import lax

D = 7168
HEADS = 64
NOPE = 128
ROPE = 64
LATENT = 512
VDIM = 128
EXP_HID = 1024
TOP = 4
TOK_DEV = 128
TOKENS = 1024
EXPERTS = 8
CAP = 128
N_CTX = 8
N_TP = 4


def draw_x_resid(key, part):
    key = jax.random.fold_in(key, 5)
    first_key = jax.random.fold_in(key, 0)
    col_frac = (jnp.arange(D, dtype=jnp.float32) + 0.5) / D
    noise = jax.random.truncated_normal(first_key, -6.0, 6.0, (TOKENS, D), jnp.float32)
    return (noise * (0.25 + 0.5 * col_frac)[None, :]).astype(jnp.bfloat16)


def draw_query_rope(key, part):
    key = jax.random.fold_in(key, 7)
    return jax.random.truncated_normal(key, -8.0, 8.0, (TOKENS, HEADS * ROPE), jnp.float32).astype(jnp.bfloat16)


def draw_key_rope(key, part):
    key = jax.random.fold_in(key, 9)
    return jax.random.truncated_normal(key, -8.0, 8.0, (ROPE, TOKENS), jnp.float32).astype(jnp.bfloat16)


def block_scale(rng, shape, pieces, least, top_value):
    def one(dim, blocks):
        draws = jax.random.uniform(jax.random.fold_in(jax.random.fold_in(rng, 6), dim), (blocks,), jnp.float32, least / len(pieces), top_value / len(pieces))
        return jnp.repeat(jnp.exp(draws), shape[dim] // blocks).reshape((-1,) + (1,) * (len(shape) - dim - 1))

    factor_of = one(*pieces[0])
    for cut in pieces[1:]:
        factor_of = factor_of * one(*cut)
    return factor_of


def routed_block(rng, own, number, rows, amount, top, bound, slope):
    ranking = jax.random.permutation(rng, amount)
    packed, usual = shares(amount, rows * top, bound, slope, True), shares(amount, rows * top, bound, slope, False)
    places = jnp.arange(amount)

    def named(tallies, turn):
        used = int((tallies > 0).sum())
        fixed = max(1, used // 4)
        passed = fixed + (places - fixed + turn * (used - fixed)) % max(1, amount - fixed)
        return jnp.zeros((amount,), jnp.int32).at[ranking[jnp.where(places < fixed, places, passed)]].set(jnp.asarray(tallies, jnp.int32))

    tallies = jnp.where(number % 4 == 0, named(packed, number // 4), named(usual, number - number // 4 - 1))
    mixed = jax.random.permutation(jax.random.fold_in(own, 3), amount)
    giver, receiver = mixed[0:amount // 2 * 2:2], mixed[1:amount // 2 * 2:2]
    margin = jnp.minimum(tallies[giver] - 1, bound - tallies[receiver]) // 2
    margin = jnp.where((giver == ranking[0]) | (receiver == ranking[0]) | (tallies[receiver] == 0), 0, jnp.maximum(margin, 0))
    passed = jax.random.randint(jax.random.fold_in(own, 4), (amount // 2,), 0, 1 << 20) % (margin + 1)
    tallies = tallies.at[giver].add(-passed).at[receiver].add(passed)
    members = jnp.searchsorted(jnp.cumsum(tallies), jnp.arange(rows * top), side="right").astype(jnp.int32)
    table = members.reshape(top, rows).T
    table = table[jax.random.permutation(jax.random.fold_in(own, 1), rows)]
    turn = jax.random.randint(jax.random.fold_in(own, 2), (rows, 1), 0, top)
    return jnp.take_along_axis(table, (jnp.arange(top)[None, :] + turn) % top, axis=1)


def shares(number_of, total, limit, slope, full):
    weights = [(1 << 20) // math.isqrt(standing ** slope) + 1 for standing in range(1, number_of + 1)]
    largest = limit if full else min(limit, max(-(-total // number_of), total * weights[0] // sum(weights)))
    least = 1 if total - largest >= number_of - 1 else 0
    counts, rest = [largest] + [least] * (number_of - 1), total - largest - least * (number_of - 1)
    while rest > 0:
        free = [i for i in range(1, number_of) if counts[i] < largest] or [i for i in range(1, number_of) if counts[i] < limit]
        mass, budget = sum([weights[i] for i in free]), rest
        for i in free:
            more = min(limit - counts[i], max(1, budget * weights[i] // mass), rest)
            counts[i] = counts[i] + more
            rest = rest - more
    return np.array(counts)


def gaussian(key, shape, width, most, cuts=(), kind=jnp.bfloat16):
    values = width * jax.random.normal(key, shape, jnp.float32)
    if cuts:
        values = values * block_scale(key, shape, cuts, -0.22, 0.18)
    return jnp.clip(values, -most, most).astype(kind)


def setup_inputs(seed: int = 0) -> dict:
    key_of = jax.random.split(jax.random.key(seed), 15)
    x_resid = draw_x_resid(jax.random.fold_in(key_of[14], 71), 0)
    query_nope = gaussian(key_of[1], (TOKENS, HEADS * NOPE), 1.0, 6.0, ((0, 8), (1, 4)))
    query_rope = draw_query_rope(jax.random.fold_in(key_of[14], 71), 0)
    latent_kv = gaussian(key_of[3], (LATENT, TOKENS), 1.0, 6.0, ((1, 8),))
    key_rope = draw_key_rope(jax.random.fold_in(key_of[14], 71), 0)
    absorb_key = gaussian(key_of[5], (HEADS, NOPE, LATENT), NOPE ** -0.5, 0.5, ((0, 4),))
    absorb_value = gaussian(key_of[6], (HEADS, LATENT, VDIM), LATENT ** -0.5, 0.25, ((0, 4),))
    out_proj = gaussian(key_of[7], (HEADS * VDIM, D), (HEADS * VDIM) ** -0.5, 0.0625, ((0, 4),))
    norm_gain = jnp.clip(1.0 + 0.18 * jax.random.normal(key_of[8], (D,), jnp.float32), 0.099609375, 1.8984375).astype(jnp.bfloat16)
    router = gaussian(key_of[9], (EXPERTS, D), D ** -0.5, 0.0625)
    routes_keys = jax.random.split(jax.random.fold_in(key_of[10], 1), TOKENS // TOK_DEV)
    routes_turns = jax.random.permutation(jax.random.fold_in(key_of[10], 3), TOKENS // TOK_DEV)
    routes = jax.vmap(lambda own, number: routed_block(jax.random.fold_in(key_of[10], 2), own, number, TOK_DEV, EXPERTS, TOP, CAP, 2))(routes_keys, routes_turns).reshape((TOKENS, TOP))
    gate_proj = gaussian(key_of[11], (EXPERTS, D, EXP_HID), D ** -0.5, 0.0625, ((0, 8), (2, 4)))
    up_proj = gaussian(key_of[12], (EXPERTS, D, EXP_HID), D ** -0.5, 0.0625, ((0, 8), (2, 4)))
    down_proj = gaussian(key_of[13], (EXPERTS, EXP_HID, D), EXP_HID ** -0.5, 0.1875, ((0, 8), (1, 4)))
    return dict(x_resid=x_resid, query_nope=query_nope, query_rope=query_rope, latent_kv=latent_kv, key_rope=key_rope, absorb_key=absorb_key, absorb_value=absorb_value, out_proj=out_proj, norm_gain=norm_gain, router=router, routes=routes, gate_proj=gate_proj, up_proj=up_proj, down_proj=down_proj)


EPS = 1e-06
ROUTE_SCALE = 2.5
LOW_SCORE = -1e+30

def reference(x_resid, query_nope, query_rope, latent_kv, key_rope, absorb_key, absorb_value, out_proj, norm_gain, router, routes, gate_proj, up_proj, down_proj):
    row_count = x_resid.shape[0]
    head_count = absorb_key.shape[0]
    query_lat = jnp.einsum('thn,hnl->thl', query_nope.reshape(row_count, head_count, NOPE).astype(jnp.float32), absorb_key.astype(jnp.float32))
    query_lat = lax.optimization_barrier(query_lat.astype(jnp.bfloat16)).astype(jnp.float32)
    query_rot = query_rope.reshape(row_count, head_count, ROPE).astype(jnp.float32)
    score_scale = (NOPE + ROPE) ** (-0.5)
    query_pos = jnp.arange(row_count, dtype=jnp.int32)

    def key_block(state, block_index):
        running, norm_sum, weighted = state
        key_begin = block_index * TOK_DEV
        latent = lax.dynamic_slice_in_dim(latent_kv, key_begin, TOK_DEV, 1).astype(jnp.float32)
        rotary = lax.dynamic_slice_in_dim(key_rope, key_begin, TOK_DEV, 1).astype(jnp.float32)
        scores = jnp.einsum('thl,ls->ths', query_lat, latent) + jnp.einsum('thr,rs->ths', query_rot, rotary)
        scores = scores * score_scale
        key_pos = key_begin + jnp.arange(TOK_DEV, dtype=jnp.int32)
        allowed = (key_pos[None, :] <= query_pos[:, None])[:, None, :]
        new_max = jnp.maximum(running, lax.optimization_barrier(jnp.max(jnp.where(allowed, scores, LOW_SCORE), axis=2)))
        exp_scores = jnp.where(allowed, jnp.exp(scores - new_max[:, :, None]), 0.0)
        factor = jnp.exp(running - new_max)
        norm_sum = norm_sum * factor + lax.optimization_barrier(jnp.sum(exp_scores, axis=2))
        rounded = lax.optimization_barrier(exp_scores.astype(jnp.bfloat16)).astype(jnp.float32)
        weighted = weighted * factor[:, :, None] + jnp.einsum('ths,ls->thl', rounded, latent)
        return ((new_max, norm_sum, weighted), None)
    start_state = (jnp.full((row_count, head_count), LOW_SCORE, jnp.float32), jnp.zeros((row_count, head_count), jnp.float32), jnp.zeros((row_count, head_count, LATENT), jnp.float32))
    final_state, _ = lax.scan(key_block, start_state, jnp.arange(N_CTX, dtype=jnp.int32))
    running, norm_sum, weighted = final_state
    attn_lat = weighted / norm_sum[:, :, None]
    attn_lat = lax.optimization_barrier(attn_lat.astype(jnp.bfloat16)).astype(jnp.float32)
    heads_out = jnp.einsum('thl,hlv->thv', attn_lat, absorb_value.astype(jnp.float32)).astype(jnp.bfloat16)
    attn_sum = jnp.dot(heads_out.reshape(row_count, head_count * VDIM), out_proj, preferred_element_type=jnp.float32)
    residual = x_resid.astype(jnp.float32) + attn_sum
    inv_rms = lax.rsqrt(lax.optimization_barrier(jnp.mean(residual * residual, axis=1)) + EPS)
    normed = residual * inv_rms[:, None] * norm_gain.astype(jnp.float32)[None, :]
    logits = jnp.dot(normed, router.astype(jnp.float32).T, precision=lax.Precision.HIGHEST)
    normed_rows = normed.astype(jnp.bfloat16)
    expert_ids = jnp.arange(EXPERTS, dtype=jnp.int32)
    onehot = routes[:, :, None] == expert_ids[None, None, :]
    chosen = lax.optimization_barrier(jnp.sum(jnp.where(onehot, logits[:, None, :], 0.0), axis=2))
    gate_vals = jax.nn.sigmoid(chosen)
    gate_vals = ROUTE_SCALE * gate_vals / lax.optimization_barrier(jnp.sum(gate_vals, axis=1, keepdims=True))
    hit_flags = onehot.astype(jnp.int32).reshape(N_CTX, TOK_DEV * TOP, EXPERTS)
    before = jnp.cumsum(hit_flags, axis=1).astype(jnp.int32) - hit_flags
    slot_ids = lax.optimization_barrier(jnp.sum(before * hit_flags, axis=2)).astype(jnp.int32).reshape(row_count * TOP)
    sources = jnp.arange(row_count * TOP, dtype=jnp.int32) // (TOK_DEV * TOP)
    places = (routes.reshape(row_count * TOP).astype(jnp.int32) * (N_CTX * CAP) + sources * CAP + slot_ids).astype(jnp.int32)
    buffer = jnp.zeros((EXPERTS * N_CTX * CAP, D), jnp.bfloat16).at[places].set(jnp.repeat(normed_rows, TOP, axis=0))
    buffer = buffer.reshape(EXPERTS, N_CTX * CAP, D)
    group_size = EXP_HID // N_TP

    def one_expert(expert_pack):
        slot_rows, gate_mat, up_mat, down_mat = expert_pack
        gate_part = jnp.dot(slot_rows, gate_mat, preferred_element_type=jnp.float32)
        up_part = jnp.dot(slot_rows, up_mat, preferred_element_type=jnp.float32)
        hidden = (jax.nn.silu(gate_part) * up_part).astype(jnp.bfloat16)
        summed = jnp.zeros((slot_rows.shape[0], D), jnp.float32)
        for group_index in range(N_TP):
            lower = group_index * group_size
            partial_term = jnp.dot(hidden[:, lower:lower + group_size], down_mat[lower:lower + group_size], preferred_element_type=jnp.float32)
            summed = summed + lax.optimization_barrier(partial_term.astype(jnp.bfloat16)).astype(jnp.float32)
        return summed.astype(jnp.bfloat16)
    outputs = lax.map(one_expert, (buffer, gate_proj, up_proj, down_proj))
    picked = outputs.reshape(EXPERTS * N_CTX * CAP, D)[places].reshape(row_count, TOP, D)
    routed_sum = lax.optimization_barrier(jnp.sum(gate_vals[:, :, None] * picked.astype(jnp.float32), axis=1))
    return (residual + routed_sum).astype(jnp.bfloat16)
```

```python
import jax
import jax.numpy as jnp
from jax import lax
from jax.sharding import PartitionSpec as P

NOPE = 128
ROPE = 64
VDIM = 128
TOP = 4
CORES = 2
DEPTH = 4


EPS = 1e-06
ROUTE_SCALE = 2.5
LOW_SCORE = -1e30


def move(value, axis, outer, inner, d_outer, d_inner):
    pairs = []
    for o in range(outer):
        for i in range(inner):
            target = (o + d_outer) % outer * inner + (i + d_inner) % inner
            pairs.append((o * inner + i, target))
    return lax.ppermute(value, axis, pairs)


def body(
    x_resid,
    query_nope,
    query_rope,
    latent_kv,
    key_rope,
    absorb_key,
    absorb_value,
    out_proj,
    norm_gain,
    router,
    routes,
    gate_proj,
    up_proj,
    down_proj,
):
    row_count = x_resid.shape[0]
    col_width = x_resid.shape[1]
    head_count = absorb_key.shape[0]
    hid = gate_proj.shape[2]
    n_ctx = lax.axis_size("ctx")
    n_tp = lax.axis_size("tp")
    expert_count = n_ctx
    nz = DEPTH if n_ctx % DEPTH == 0 else 1
    nx = n_ctx // nz
    nc = CORES if n_tp % CORES == 0 else 1
    ny = n_tp // nc
    model_width = col_width * n_tp
    ctx = lax.axis_index("ctx")
    tp = lax.axis_index("tp")
    my_z, my_x = ctx // nx, ctx % nx
    my_y, my_c = tp // nc, tp % nc
    col_start = tp * col_width

    def over_ctx(value, dz, dx):
        return move(value, "ctx", nz, nx, dz, dx)

    def over_tp(value, dy, dc):
        return move(value, "tp", ny, nc, dy, dc)

    def tp_at(dy, dc):
        return (my_y + dy) % ny * nc + (my_c + dc) % nc

    def gather_ctx(value):
        column = [value]
        for _ in range(nz - 1):
            column.append(over_ctx(column[-1], 1, 0))
        return [[b] + [over_ctx(b, 0, dx) for dx in range(1, nx)] for b in column]

    keys = jnp.concatenate([latent_kv, key_rope], axis=0)
    key_blocks = gather_ctx(keys)

    gate_up = {}
    down = {}
    for dy in range(ny):
        for dc in range(nc):
            begin = tp_at(dy, dc) * col_width
            piece = jnp.concatenate(
                [
                    lax.dynamic_slice_in_dim(gate_proj[0], begin, col_width, 0),
                    lax.dynamic_slice_in_dim(up_proj[0], begin, col_width, 0),
                ],
                axis=1,
            )
            gate_up[dy, dc] = over_tp(piece, dy, dc) if (dy or dc) else piece
    for dy in range(ny):
        for dc in range(nc):
            begin = tp_at(dy, dc) * col_width
            piece = lax.dynamic_slice_in_dim(down_proj[0], begin, col_width, 1)
            down[dy, dc] = over_tp(piece, dy, dc) if (dy or dc) else piece

    query_pos = ctx * row_count + jnp.arange(row_count, dtype=jnp.int32)
    query_lat = jnp.einsum(
        "thn,hnl->thl",
        query_nope.reshape(row_count, head_count, NOPE),
        absorb_key,
        preferred_element_type=jnp.float32,
    ).astype(jnp.bfloat16)
    query_rot = query_rope.reshape(row_count, head_count, ROPE)
    score_scale = (NOPE + ROPE) ** (-0.5)
    all_keys = jnp.concatenate([b for line in key_blocks for b in line], axis=1)
    latent, rotary = all_keys[: latent_kv.shape[0]], all_keys[latent_kv.shape[0] :]
    owners = jnp.stack(
        [(my_z - dz) % nz * nx + (my_x - dx) % nx for dz in range(nz) for dx in range(nx)]
    )
    key_pos = (
        owners[:, None].astype(jnp.int32) * row_count
        + jnp.arange(row_count, dtype=jnp.int32)[None, :]
    ).reshape(n_ctx * row_count)
    scores = jnp.einsum("thl,ls->ths", query_lat, latent, preferred_element_type=jnp.float32)
    scores = (
        scores + jnp.einsum("thr,rs->ths", query_rot, rotary, preferred_element_type=jnp.float32)
    ) * score_scale
    allowed = (key_pos[None, :] <= query_pos[:, None])[:, None, :]
    top_score = jnp.max(jnp.where(allowed, scores, LOW_SCORE), axis=2)
    exp_scores = jnp.where(allowed, jnp.exp(scores - top_score[:, :, None]), 0.0)
    norm_sum = jnp.sum(exp_scores, axis=2)
    weighted = jnp.einsum(
        "ths,ls->thl", exp_scores.astype(jnp.bfloat16), latent, preferred_element_type=jnp.float32
    )
    attn_lat = (weighted / norm_sum[:, :, None]).astype(jnp.bfloat16)
    heads_out = jnp.einsum(
        "thl,hlv->thv", attn_lat, absorb_value, preferred_element_type=jnp.float32
    ).astype(jnp.bfloat16)
    attn_part = jnp.dot(
        heads_out.reshape(row_count, head_count * VDIM),
        out_proj,
        preferred_element_type=jnp.float32,
    )

    def own_part(dy, dc):
        return lax.dynamic_slice_in_dim(attn_part, tp_at(dy, dc) * col_width, col_width, 1)

    held = {dy: own_part(dy, 0) for dy in range(ny)}
    for dc in range(1, nc):
        for dy in range(ny):
            held[dy] = held[dy] + over_tp(own_part(dy, dc).astype(jnp.bfloat16), 0, dc).astype(
                jnp.float32
            )
    residual = x_resid.astype(jnp.float32) + held[0]
    for dy in range(1, ny):
        residual = residual + over_tp(held[dy].astype(jnp.bfloat16), dy, 0).astype(jnp.float32)

    gain = lax.dynamic_slice_in_dim(norm_gain, col_start, col_width, 0).astype(jnp.float32)
    scaled = residual * gain[None, :]
    token_blocks = gather_ctx(scaled.astype(jnp.bfloat16))

    router_cols = lax.dynamic_slice_in_dim(router, col_start, col_width, 1).astype(jnp.float32)
    stats = jnp.concatenate(
        [
            lax.dot_general(
                router_cols, scaled, (((1,), (1,)), ((), ())), precision=lax.Precision.HIGHEST
            ),
            jnp.sum(residual * residual, axis=1)[None, :],
        ],
        axis=0,
    )
    for dc in range(1, nc):
        stats = stats + over_tp(stats, 0, dc) if nc == 2 else stats
    stats = sum([over_tp(stats, dy, 0) for dy in range(1, ny)], stats)
    inv_rms = lax.rsqrt(stats[expert_count] / model_width + EPS)
    logits = stats[:expert_count] * inv_rms[None, :]
    expert_ids = jnp.arange(expert_count, dtype=jnp.int32)
    onehot = routes.T[:, None, :] == expert_ids[None, :, None]
    chosen = jnp.sum(jnp.where(onehot, logits[None, :, :], 0.0), axis=1)
    gate_vals = jax.nn.sigmoid(chosen)
    gate_vals = ROUTE_SCALE * gate_vals / jnp.sum(gate_vals, axis=0, keepdims=True)
    dense_gates = jnp.sum(jnp.where(onehot, gate_vals[:, None, :], 0.0), axis=0)
    meta_blocks = gather_ctx(jnp.concatenate([dense_gates, inv_rms[None, :]], axis=0))

    down_mat = jnp.concatenate(
        [down[dy, dc] for dc in range(nc) for dy in range(ny)], axis=0
    )

    def experts(dz):
        rows = jnp.concatenate(token_blocks[dz], axis=0)
        meta = jnp.concatenate(meta_blocks[dz], axis=1)
        row_scale = meta[expert_count][:, None]
        row_gate = lax.dynamic_slice_in_dim(meta, ctx, 1, 0)[0][:, None]

        def product(dy, dc):
            return jnp.dot(rows, gate_up[dy, dc], preferred_element_type=jnp.float32)

        sums = [None] * ny
        for dc in list(range(1, nc)):
            away = jnp.concatenate(
                [product(dy, dc).astype(jnp.bfloat16) for dy in range(ny)], axis=1
            )
            away = over_tp(away, 0, -dc).astype(jnp.float32)
            for dy in range(ny):
                term = away[:, dy * 2 * hid : (dy + 1) * 2 * hid]
                sums[dy] = term if sums[dy] is None else sums[dy] + term
        for dy in range(ny):
            mine = product(dy, 0)
            sums[dy] = mine if sums[dy] is None else sums[dy] + mine
        total = sums[0]
        for dy in range(1, ny):
            total = total + over_tp(sums[dy].astype(jnp.bfloat16), -dy, 0).astype(jnp.float32)
        total = total * row_scale
        hidden = (jax.nn.silu(total[:, :hid]) * total[:, hid:]).astype(jnp.bfloat16)
        line = jnp.concatenate(
            [hidden] + [over_tp(hidden, dy, 0) for dy in range(1, ny)], axis=1
        )
        whole = jnp.concatenate([line] + [over_tp(line, 0, dc) for dc in range(1, nc)], axis=1)
        out = jnp.dot(whole, down_mat, preferred_element_type=jnp.float32) * row_gate
        acc = out[:row_count]
        for dx in range(1, nx):
            other = out[dx * row_count : (dx + 1) * row_count].astype(jnp.bfloat16)
            acc = acc + over_ctx(other, 0, -dx).astype(jnp.float32)
        return acc

    parts = [experts(dz) for dz in range(nz)]
    total = None
    for dz in list(range(1, nz)):
        total = parts[dz] if total is None else total + parts[dz]
        total = over_ctx(total.astype(jnp.bfloat16), 1, 0).astype(jnp.float32)
    routed_sum = parts[0] if total is None else total + parts[0]
    return (residual + routed_sum).astype(jnp.bfloat16)


def solution(mesh):
    return jax.shard_map(
        body,
        mesh=mesh,
        in_specs=(
            P("ctx", "tp"),
            P("ctx", "tp"),
            P("ctx", "tp"),
            P(None, "ctx"),
            P(None, "ctx"),
            P("tp", None, None),
            P("tp", None, None),
            P("tp", None),
            P(),
            P(),
            P("ctx", None),
            P("ctx", None, "tp"),
            P("ctx", None, "tp"),
            P("ctx", "tp", None),
        ),
        out_specs=P("ctx", "tp"),
        check_vma=False,
    )
```

```python
import functools

import jax
import jax.numpy as jnp
from jax import lax
from jax.experimental import pallas as pl
from jax.experimental.pallas import tpu as pltpu
from jax.sharding import PartitionSpec as P

NOPE = 128
ROPE = 64
VDIM = 128
TOP = 4
CORES = 2
DEPTH = 4
META = 128


EPS = 1e-06
ROUTE_SCALE = 2.5
LOW_SCORE = -1e30


def move(value, axis, outer, inner, d_outer, d_inner):
    pairs = []
    for o in range(outer):
        for i in range(inner):
            target = (o + d_outer) % outer * inner + (i + d_inner) % inner
            pairs.append((o * inner + i, target))
    return lax.ppermute(value, axis, pairs)


def body(
    x_resid,
    query_nope,
    query_rope,
    latent_kv,
    key_rope,
    absorb_key,
    absorb_value,
    out_proj,
    norm_gain,
    router,
    routes,
    gate_proj,
    up_proj,
    down_proj,
):
    row_count = x_resid.shape[0]
    col_width = x_resid.shape[1]
    head_count = absorb_key.shape[0]
    hid = gate_proj.shape[2]
    n_ctx = lax.axis_size("ctx")
    n_tp = lax.axis_size("tp")
    expert_count = n_ctx
    nz = DEPTH if n_ctx % DEPTH == 0 else 1
    nx = n_ctx // nz
    nc = CORES if n_tp % CORES == 0 else 1
    ny = n_tp // nc
    model_width = col_width * n_tp
    ctx = lax.axis_index("ctx")
    tp = lax.axis_index("tp")
    my_z, my_x = ctx // nx, ctx % nx
    my_y, my_c = tp // nc, tp % nc
    col_start = tp * col_width

    def over_ctx(value, dz, dx):
        return move(value, "ctx", nz, nx, dz, dx)

    def over_tp(value, dy, dc):
        return move(value, "tp", ny, nc, dy, dc)

    def tp_at(dy, dc):
        return (my_y + dy) % ny * nc + (my_c + dc) % nc

    def gather_ctx(value):
        column = [value]
        for _ in range(nz - 1):
            column.append(over_ctx(column[-1], 1, 0))
        return [[b] + [over_ctx(b, 0, dx) for dx in range(1, nx)] for b in column]

    keys = jnp.concatenate([latent_kv, key_rope], axis=0)
    key_blocks = gather_ctx(keys)

    def exchanged(weight, dy, dc):
        piece = lax.dynamic_slice_in_dim(weight[0], tp_at(dy, dc) * col_width, col_width, 0)
        return over_tp(piece, dy, dc) if (dy or dc) else piece

    offsets = [(dy, dc) for dc in range(nc) for dy in range(ny)]
    gates = [exchanged(gate_proj, dy, dc) for dy, dc in offsets]
    ups = [exchanged(up_proj, dy, dc) for dy, dc in offsets]

    query_pos = ctx * row_count + jnp.arange(row_count, dtype=jnp.int32)
    query_lat = jnp.einsum(
        "thn,hnl->thl",
        query_nope.reshape(row_count, head_count, NOPE),
        absorb_key,
        preferred_element_type=jnp.float32,
    ).astype(jnp.bfloat16)
    query_lat, *gates = lax.optimization_barrier((query_lat, *gates))
    query_rot = query_rope.reshape(row_count, head_count, ROPE)
    score_scale = (NOPE + ROPE) ** (-0.5)
    all_keys = jnp.concatenate([b for line in key_blocks for b in line], axis=1)
    latent, rotary = all_keys[: latent_kv.shape[0]], all_keys[latent_kv.shape[0] :]
    owners = jnp.stack(
        [(my_z - dz) % nz * nx + (my_x - dx) % nx for dz in range(nz) for dx in range(nx)]
    )
    key_pos = (
        owners[:, None].astype(jnp.int32) * row_count
        + jnp.arange(row_count, dtype=jnp.int32)[None, :]
    ).reshape(n_ctx * row_count)
    scores = jnp.einsum("thl,ls->ths", query_lat, latent, preferred_element_type=jnp.float32)
    scores = (
        scores + jnp.einsum("thr,rs->ths", query_rot, rotary, preferred_element_type=jnp.float32)
    ) * score_scale
    allowed = (key_pos[None, :] <= query_pos[:, None])[:, None, :]
    top_score = jnp.max(jnp.where(allowed, scores, LOW_SCORE), axis=2)
    exp_scores = jnp.where(allowed, jnp.exp(scores - top_score[:, :, None]), 0.0)
    norm_sum = jnp.sum(exp_scores, axis=2)
    weighted = jnp.einsum(
        "ths,ls->thl", exp_scores.astype(jnp.bfloat16), latent, preferred_element_type=jnp.float32
    )
    attn_lat = (weighted / norm_sum[:, :, None]).astype(jnp.bfloat16)
    heads_out = jnp.einsum(
        "thl,hlv->thv", attn_lat, absorb_value, preferred_element_type=jnp.float32
    ).astype(jnp.bfloat16)
    heads_out, *ups = lax.optimization_barrier((heads_out, *ups))
    attn_part = jnp.dot(
        heads_out.reshape(row_count, head_count * VDIM),
        out_proj,
        preferred_element_type=jnp.float32,
    )

    def own_part(dy, dc):
        return lax.dynamic_slice_in_dim(attn_part, tp_at(dy, dc) * col_width, col_width, 1)

    held = {dy: own_part(dy, 0) for dy in range(ny)}
    for dc in range(1, nc):
        for dy in range(ny):
            held[dy] = held[dy] + over_tp(own_part(dy, dc).astype(jnp.bfloat16), 0, dc).astype(
                jnp.float32
            )
    residual = x_resid.astype(jnp.float32) + held[0]
    for dy in range(1, ny):
        residual = residual + over_tp(held[dy].astype(jnp.bfloat16), dy, 0).astype(jnp.float32)

    gain = lax.dynamic_slice_in_dim(norm_gain, col_start, col_width, 0).astype(jnp.float32)
    scaled = residual * gain[None, :]

    router_cols = lax.dynamic_slice_in_dim(router, col_start, col_width, 1).astype(jnp.float32)
    stats = jnp.concatenate(
        [
            lax.dot_general(
                router_cols, scaled, (((1,), (1,)), ((), ())), precision=lax.Precision.HIGHEST
            ),
            jnp.sum(residual * residual, axis=1)[None, :],
        ],
        axis=0,
    )
    stats = sum([over_tp(stats, 0, dc) for dc in range(1, nc)], stats)
    stats = sum([over_tp(stats, dy, 0) for dy in range(1, ny)], stats)
    inv_rms = lax.rsqrt(stats[expert_count] / model_width + EPS)
    logits = stats[:expert_count] * inv_rms[None, :]
    expert_ids = jnp.arange(expert_count, dtype=jnp.int32)
    onehot = routes.T[:, None, :] == expert_ids[None, :, None]
    chosen = jnp.sum(jnp.where(onehot, logits[None, :, :], 0.0), axis=1)
    gate_vals = jax.nn.sigmoid(chosen)
    gate_vals = ROUTE_SCALE * gate_vals / jnp.sum(gate_vals, axis=0, keepdims=True)
    dense_gates = jnp.sum(jnp.where(onehot, gate_vals[:, None, :], 0.0), axis=0)
    tokens = (scaled * inv_rms[:, None]).astype(jnp.bfloat16)
    high = dense_gates.T.astype(jnp.bfloat16)
    low = (dense_gates.T - high.astype(jnp.float32)).astype(jnp.bfloat16)
    fill = jnp.zeros((row_count, META // 2 - expert_count), jnp.bfloat16)
    packet = jnp.concatenate([tokens, high, fill, low, fill], axis=1)
    routed_sum = expert_call((nz, nx, ny, nc), packet, gates, ups, down_proj[0])
    return (residual + routed_sum).astype(jnp.bfloat16)


def expert_kernel(dims, *refs):
    nz, nx, ny, nc = dims
    n_tp = ny * nc
    packet, refs = refs[0], refs[1:]
    gates, ups, refs = refs[:n_tp], refs[n_tp : 2 * n_tp], refs[2 * n_tp :]
    down, out = refs[0], refs[1]
    (tok, dmat, own, core_out, core_in, y_out, y_in, hid, acc, x_out, x_in, z_out, z_in) = refs[2:15]
    (s_z, r_z, s_x, r_x, s_d, r_d, s_c, r_c, s_y, r_y) = refs[15:25]
    (s_hy, r_hy, s_hc, r_hc, s_bx, r_bx, s_bz, r_bz, local_sem) = refs[25:]
    rows, width = out.shape
    h = down.shape[0]
    ctx, tp = lax.axis_index("ctx"), lax.axis_index("tp")
    z, x, y, c = ctx // nx, ctx % nx, tp // nc, tp % nc

    def ctx_at(dz, dx):
        return ((z + dz + nz) % nz * nx + (x + dx + nx) % nx, tp)

    def tp_at(dy, dc):
        return (ctx, (y + dy + ny) % ny * nc + (c + dc + nc) % nc)

    def push(src, dst, send, recv, where):
        copy = pltpu.make_async_remote_copy(
            src_ref=src,
            dst_ref=dst,
            send_sem=send,
            recv_sem=recv,
            device_id=where,
            device_id_type=pl.DeviceIdType.MESH,
        )
        copy.start()
        return copy

    peers = [ctx_at(0, dx) for dx in range(1, nx)]
    if nz > 1:
        peers.append(ctx_at(1, 0))
    if nz > 2:
        peers.append(ctx_at(-1, 0))
    peers += [tp_at(dy, dc) for dc in range(nc) for dy in range(ny) if dy or dc]
    barrier = pltpu.get_barrier_semaphore()
    for peer in peers:
        pl.semaphore_signal(
            barrier, inc=1, device_id=peer, device_id_type=pl.DeviceIdType.MESH
        )
    pl.semaphore_wait(barrier, len(peers))

    sent = []
    zc, xc, dcp, cc, yc, hyc, hcc, bxc, bzc = ({} for _ in range(9))

    def pass_on(dz):
        block = packet if dz == 0 else tok.at[dz, pl.ds(0, rows)]
        if dz:
            zc[dz].wait_recv()
        if dz + 1 < nz:
            zc[dz + 1] = push(
                block, tok.at[dz + 1, pl.ds(0, rows)], s_z.at[dz], r_z.at[dz], ctx_at(1, 0)
            )
            sent.append(zc[dz + 1])
        for dx in range(1, nx):
            xc[dz, dx] = push(
                block,
                tok.at[dz, pl.ds(dx * rows, rows)],
                s_x.at[dz, dx - 1],
                r_x.at[dz, dx - 1],
                ctx_at(0, dx),
            )
            sent.append(xc[dz, dx])

    def down_cols(dy, dc):
        begin = tp_at(dy, dc)[1] * width
        return down.at[:, pl.ds(pl.multiple_of(begin, 128), width)]

    pass_on(0)
    mine = pltpu.make_async_copy(down_cols(0, 0), dmat.at[pl.ds(0, h)], local_sem)
    mine.start()
    for dc in range(nc - 1, -1, -1):
        for dy in range(ny):
            if dy or dc:
                k = dc * ny + dy
                dcp[k] = push(
                    down_cols(dy, dc),
                    dmat.at[pl.ds(k * h, h)],
                    s_d.at[k - 1],
                    r_d.at[k - 1],
                    tp_at(dy, dc),
                )
                sent.append(dcp[k])
    tok[0, pl.ds(0, rows), :] = packet[...]

    def products(dz):
        for dx in range(1, nx):
            xc[dz, dx].wait_recv()
        for dc in range(nc - 1, -1, -1):
            for dy in range(ny):
                k = dc * ny + dy
                for part, weight in enumerate((gates[k], ups[k])):
                    value = jnp.dot(
                        tok[dz, :, pl.ds(0, width)],
                        weight[...],
                        preferred_element_type=jnp.float32,
                    )
                    if dc:
                        lanes = pl.ds((2 * dy + part) * h, h)
                        core_out[dz, dc - 1, :, lanes] = value.astype(jnp.bfloat16)
                    else:
                        own[dz, dy, :, pl.ds(part * h, h)] = value
            if dc:
                cc[dz, dc] = push(
                    core_out.at[dz, dc - 1],
                    core_in.at[dz, dc - 1],
                    s_c.at[dz, dc - 1],
                    r_c.at[dz, dc - 1],
                    tp_at(0, -dc),
                )
                sent.append(cc[dz, dc])

    def chip_sums(dz):
        for dc in range(1, nc):
            cc[dz, dc].wait_recv()
        for dy in list(range(1, ny)) + [0]:
            value = own[dz, dy]
            for dc in range(1, nc):
                value = value + core_in[dz, dc - 1, :, pl.ds(2 * dy * h, 2 * h)].astype(jnp.float32)
            if dy:
                y_out[dz, dy - 1] = value.astype(jnp.bfloat16)
                yc[dz, dy] = push(
                    y_out.at[dz, dy - 1],
                    y_in.at[dz, dy - 1],
                    s_y.at[dz, dy - 1],
                    r_y.at[dz, dy - 1],
                    tp_at(-dy, 0),
                )
                sent.append(yc[dz, dy])
            else:
                own[dz, 0] = value

    def activate(dz):
        value = own[dz, 0]
        for dy in range(1, ny):
            yc[dz, dy].wait_recv()
            value = value + y_in[dz, dy - 1].astype(jnp.float32)
        gate, up = value[:, :h], value[:, h:]
        hid[dz, :, pl.ds(0, h)] = (gate / (1.0 + jnp.exp(-gate)) * up).astype(jnp.bfloat16)
        for dy in range(1, ny):
            hyc[dz, dy] = push(
                hid.at[dz, :, pl.ds(0, h)],
                hid.at[dz, :, pl.ds(dy * h, h)],
                s_hy.at[dz, dy - 1],
                r_hy.at[dz, dy - 1],
                tp_at(dy, 0),
            )
            sent.append(hyc[dz, dy])

    def share_hidden(dz):
        for dy in range(1, ny):
            hyc[dz, dy].wait_recv()
        for dc in range(1, nc):
            hcc[dz, dc] = push(
                hid.at[dz, :, pl.ds(0, ny * h)],
                hid.at[dz, :, pl.ds(dc * ny * h, ny * h)],
                s_hc.at[dz, dc - 1],
                r_hc.at[dz, dc - 1],
                tp_at(0, dc),
            )
            sent.append(hcc[dz, dc])

    step = 256 if width % 256 == 0 else 128

    def outputs(dz, first):
        for dc in range(1, nc):
            hcc[dz, dc].wait_recv()
        if first:
            mine.wait()
            for k in dcp:
                dcp[k].wait_recv()
        meta = tok[dz, :, pl.ds(width, META)].astype(jnp.float32)
        lane = lax.broadcasted_iota(jnp.int32, meta.shape, 1)
        picked = (lane == ctx) | (lane == ctx + META // 2)
        gate = jnp.sum(jnp.where(picked, meta, 0.0), axis=1, keepdims=True)
        for j in range(width // step):
            cols = pl.ds(j * step, step)
            value = gate * jnp.dot(
                hid[dz], dmat[:, cols], preferred_element_type=jnp.float32
            )
            acc[dz, :, cols] = value[:rows]
            for dx in range(1, nx):
                x_out[dz, dx - 1, :, cols] = value[dx * rows : (dx + 1) * rows].astype(jnp.bfloat16)
        for dx in range(1, nx):
            bxc[dz, dx] = push(
                x_out.at[dz, dx - 1],
                x_in.at[dz, dx - 1],
                s_bx.at[dz, dx - 1],
                r_bx.at[dz, dx - 1],
                ctx_at(0, -dx),
            )
            sent.append(bxc[dz, dx])

    def give_back(dz):
        value = acc[dz]
        for dx in range(1, nx):
            bxc[dz, dx].wait_recv()
            value = value + x_in[dz, dx - 1].astype(jnp.float32)
        if dz != 1 and nz > 1:
            before = (dz or nz) - 1
            bzc[before].wait_recv()
            value = value + z_in[before - 1].astype(jnp.float32)
        if dz:
            z_out[dz - 1] = value.astype(jnp.bfloat16)
            bzc[dz] = push(
                z_out.at[dz - 1], z_in.at[dz - 1], s_bz.at[dz - 1], r_bz.at[dz - 1], ctx_at(1, 0)
            )
            sent.append(bzc[dz])
        else:
            out[...] = value

    for turn in range(nz + 3):
        if turn + 1 < nz:
            pass_on(turn + 1)
        if turn < nz:
            products(turn)
        if 0 <= turn - 1 < nz:
            chip_sums(turn - 1)
        if 0 <= turn - 2 < nz:
            share_hidden(turn - 2)
        if 0 <= turn - 1 < nz:
            activate(turn - 1)
        if 0 <= turn - 2 < nz:
            outputs(turn - 2, turn == 2)
        if 1 <= turn - 3 < nz:
            give_back(turn - 3)
    give_back(0)
    for copy in sent:
        copy.wait_send()


def expert_call(dims, packet, gates, ups, down):
    nz, nx, ny, nc = dims
    n_tp = ny * nc
    rows = packet.shape[0]
    width = packet.shape[1] - META
    h = down.shape[0]
    all_rows = nx * rows
    px, py, pc, pz = max(nx - 1, 1), max(ny - 1, 1), max(nc - 1, 1), max(nz - 1, 1)
    bf16, f32 = jnp.bfloat16, jnp.float32
    vmem = pl.BlockSpec(memory_space=pltpu.VMEM)
    sem = pltpu.SemaphoreType.DMA
    shapes = [
        pltpu.VMEM((nz, all_rows, width + META), bf16),
        pltpu.VMEM((n_tp * h, width), bf16),
        pltpu.VMEM((nz, ny, all_rows, 2 * h), f32),
        pltpu.VMEM((nz, pc, all_rows, ny * 2 * h), bf16),
        pltpu.VMEM((nz, pc, all_rows, ny * 2 * h), bf16),
        pltpu.VMEM((nz, py, all_rows, 2 * h), bf16),
        pltpu.VMEM((nz, py, all_rows, 2 * h), bf16),
        pltpu.VMEM((nz, all_rows, n_tp * h), bf16),
        pltpu.VMEM((nz, rows, width), f32),
        pltpu.VMEM((nz, px, rows, width), bf16),
        pltpu.VMEM((nz, px, rows, width), bf16),
        pltpu.VMEM((pz, rows, width), bf16),
        pltpu.VMEM((pz, rows, width), bf16),
    ]
    sems = []
    for shape in ((pz,), (nz, px), (n_tp,), (nz, pc), (nz, py), (nz, py), (nz, pc), (nz, px), (pz,)):
        sems += [sem(shape), sem(shape)]
    flops = 2 * nz * all_rows * width * n_tp * h * 3
    return pl.pallas_call(
        functools.partial(expert_kernel, dims),
        out_shape=jax.ShapeDtypeStruct((rows, width), f32),
        in_specs=[vmem] * (1 + 2 * n_tp) + [pl.BlockSpec(memory_space=pl.ANY)],
        out_specs=vmem,
        scratch_shapes=shapes + sems + [sem],
        compiler_params=pltpu.CompilerParams(
            collective_id=1, has_side_effects=True, vmem_limit_bytes=58 * 1024 * 1024
        ),
        cost_estimate=pl.CostEstimate(
            flops=flops, bytes_accessed=16 * 1024 * 1024, transcendentals=0
        ),
        name="experts",
    )(packet, *gates, *ups, down)


def solution(mesh):
    return jax.shard_map(
        body,
        mesh=mesh,
        in_specs=(
            P("ctx", "tp"),
            P("ctx", "tp"),
            P("ctx", "tp"),
            P(None, "ctx"),
            P(None, "ctx"),
            P("tp", None, None),
            P("tp", None, None),
            P("tp", None),
            P(),
            P(),
            P("ctx", None),
            P("ctx", None, "tp"),
            P("ctx", None, "tp"),
            P("ctx", "tp", None),
        ),
        out_specs=P("ctx", "tp"),
        check_vma=False,
    )
```

```python
import functools

import jax
import jax.numpy as jnp
from jax import lax
from jax.experimental import pallas as pl
from jax.experimental.pallas import tpu as pltpu
from jax.sharding import PartitionSpec as P

NOPE = 128
ROPE = 64
VDIM = 128
TOP = 4
CORES = 2
DEPTH = 4
META = 128


EPS = 1e-06
ROUTE_SCALE = 2.5
LOW_SCORE = -1e30


def move(value, axis, outer, inner, d_outer, d_inner):
    pairs = []
    for o in range(outer):
        for i in range(inner):
            target = (o + d_outer) % outer * inner + (i + d_inner) % inner
            pairs.append((o * inner + i, target))
    return lax.ppermute(value, axis, pairs)


def body(
    x_resid,
    query_nope,
    query_rope,
    latent_kv,
    key_rope,
    absorb_key,
    absorb_value,
    out_proj,
    norm_gain,
    router,
    routes,
    gate_proj,
    up_proj,
    down_proj,
):
    row_count = x_resid.shape[0]
    col_width = x_resid.shape[1]
    head_count = absorb_key.shape[0]
    hid = gate_proj.shape[2]
    n_ctx = lax.axis_size("ctx")
    n_tp = lax.axis_size("tp")
    expert_count = n_ctx
    nz = DEPTH if n_ctx % DEPTH == 0 else 1
    nx = n_ctx // nz
    nc = CORES if n_tp % CORES == 0 else 1
    ny = n_tp // nc
    model_width = col_width * n_tp
    ctx = lax.axis_index("ctx")
    tp = lax.axis_index("tp")
    my_z, my_x = ctx // nx, ctx % nx
    my_y, my_c = tp // nc, tp % nc
    col_start = tp * col_width

    def over_ctx(value, dz, dx):
        return move(value, "ctx", nz, nx, dz, dx)

    def over_tp(value, dy, dc):
        return move(value, "tp", ny, nc, dy, dc)

    def tp_at(dy, dc):
        return (my_y + dy) % ny * nc + (my_c + dc) % nc

    def gather_ctx(value):
        column = [value]
        for _ in range(nz - 1):
            column.append(over_ctx(column[-1], 1, 0))
        return [[b] + [over_ctx(b, 0, dx) for dx in range(1, nx)] for b in column]

    offsets = [(dy, dc) for dc in range(nc) for dy in range(ny)]

    def pieces(weight, dim):
        return [
            lax.dynamic_slice_in_dim(weight[0], tp_at(dy, dc) * col_width, col_width, dim)
            for dy, dc in offsets
        ]

    def exchange(cut):
        return [over_tp(p, *at) if at != (0, 0) else p for p, at in zip(cut, offsets)]

    latent_kv, *gate_cut = lax.optimization_barrier((latent_kv, *pieces(gate_proj, 0)))
    gates = exchange(gate_cut)
    ups = exchange(pieces(up_proj, 0))
    near = [i for i, (dy, dc) in enumerate(offsets) if not (dy and dc)]
    down_cut = [pieces(down_proj, 1)[i] for i in near]

    keys = jnp.concatenate([latent_kv, key_rope], axis=0)
    key_blocks = gather_ctx(keys)

    query_pos = ctx * row_count + jnp.arange(row_count, dtype=jnp.int32)
    query_lat = jnp.einsum(
        "thn,hnl->thl",
        query_nope.reshape(row_count, head_count, NOPE),
        absorb_key,
        preferred_element_type=jnp.float32,
    ).astype(jnp.bfloat16)
    query_lat, *gates = lax.optimization_barrier((query_lat, *gates))
    query_rot = query_rope.reshape(row_count, head_count, ROPE)
    score_scale = (NOPE + ROPE) ** (-0.5)
    all_keys = jnp.concatenate([b for line in key_blocks for b in line], axis=1)
    latent, rotary = all_keys[: latent_kv.shape[0]], all_keys[latent_kv.shape[0] :]
    owners = jnp.stack(
        [(my_z - dz) % nz * nx + (my_x - dx) % nx for dz in range(nz) for dx in range(nx)]
    )
    key_pos = (
        owners[:, None].astype(jnp.int32) * row_count
        + jnp.arange(row_count, dtype=jnp.int32)[None, :]
    ).reshape(n_ctx * row_count)
    scores = jnp.einsum("thl,ls->ths", query_lat, latent, preferred_element_type=jnp.float32)
    scores = (
        scores + jnp.einsum("thr,rs->ths", query_rot, rotary, preferred_element_type=jnp.float32)
    ) * score_scale
    allowed = (key_pos[None, :] <= query_pos[:, None])[:, None, :]
    top_score = jnp.max(jnp.where(allowed, scores, LOW_SCORE), axis=2)
    exp_scores = jnp.where(allowed, jnp.exp(scores - top_score[:, :, None]), 0.0)
    norm_sum = jnp.sum(exp_scores, axis=2)
    weighted = jnp.einsum(
        "ths,ls->thl", exp_scores.astype(jnp.bfloat16), latent, preferred_element_type=jnp.float32
    )
    attn_lat = (weighted / norm_sum[:, :, None]).astype(jnp.bfloat16)
    heads_out = jnp.einsum(
        "thl,hlv->thv", attn_lat, absorb_value, preferred_element_type=jnp.float32
    ).astype(jnp.bfloat16)
    heads_out, *rest = lax.optimization_barrier((heads_out, *ups[:-1], *down_cut))
    ups[:-1], down_cut = rest[: len(ups) - 1], rest[len(ups) - 1 :]
    downs = [over_tp(p, *offsets[i]) if i else p for p, i in zip(down_cut, near)]
    attn_part = jnp.dot(
        heads_out.reshape(row_count, head_count * VDIM),
        out_proj,
        preferred_element_type=jnp.float32,
    )

    attn_part, ups[-1] = lax.optimization_barrier((attn_part, ups[-1]))

    def own_part(dy, dc):
        return lax.dynamic_slice_in_dim(attn_part, tp_at(dy, dc) * col_width, col_width, 1)

    held = {dy: own_part(dy, 0) for dy in range(ny)}
    for dc in range(1, nc):
        for dy in range(ny):
            held[dy] = held[dy] + over_tp(own_part(dy, dc).astype(jnp.bfloat16), 0, dc).astype(
                jnp.float32
            )
    residual = x_resid.astype(jnp.float32) + held[0]
    for dy in range(1, ny):
        residual = residual + over_tp(held[dy].astype(jnp.bfloat16), dy, 0).astype(jnp.float32)

    gain = lax.dynamic_slice_in_dim(norm_gain, col_start, col_width, 0).astype(jnp.float32)
    scaled = residual * gain[None, :]

    router_cols = lax.dynamic_slice_in_dim(router, col_start, col_width, 1).astype(jnp.float32)
    stats = jnp.concatenate(
        [
            lax.dot_general(
                router_cols, scaled, (((1,), (1,)), ((), ())), precision=lax.Precision.HIGHEST
            ),
            jnp.sum(residual * residual, axis=1)[None, :],
        ],
        axis=0,
    )
    stats = sum([over_tp(stats, 0, dc) for dc in range(1, nc)], stats)
    stats = sum([over_tp(stats, dy, 0) for dy in range(1, ny)], stats)
    inv_rms = lax.rsqrt(stats[expert_count] / model_width + EPS)
    logits = stats[:expert_count] * inv_rms[None, :]
    expert_ids = jnp.arange(expert_count, dtype=jnp.int32)
    onehot = routes.T[:, None, :] == expert_ids[None, :, None]
    chosen = jnp.sum(jnp.where(onehot, logits[None, :, :], 0.0), axis=1)
    gate_vals = jax.nn.sigmoid(chosen)
    gate_vals = ROUTE_SCALE * gate_vals / jnp.sum(gate_vals, axis=0, keepdims=True)
    dense_gates = jnp.sum(jnp.where(onehot, gate_vals[:, None, :], 0.0), axis=0)
    tokens = (scaled * inv_rms[:, None]).astype(jnp.bfloat16)
    high = dense_gates.T.astype(jnp.bfloat16)
    low = (dense_gates.T - high.astype(jnp.float32)).astype(jnp.bfloat16)
    fill = jnp.zeros((row_count, META // 2 - expert_count), jnp.bfloat16)
    packet = jnp.concatenate([tokens, high, fill, low, fill], axis=1)
    routed_sum = expert_call((nz, nx, ny, nc), packet, gates, ups, downs, down_proj[0])
    return (residual + routed_sum).astype(jnp.bfloat16)


def expert_kernel(dims, *refs):
    nz, nx, ny, nc = dims
    n_tp = ny * nc
    packet, refs = refs[0], refs[1:]
    gates, ups, refs = refs[:n_tp], refs[n_tp : 2 * n_tp], refs[2 * n_tp :]
    offsets = [(dy, dc) for dc in range(nc) for dy in range(ny)]
    near = [at for at in offsets if not (at[0] and at[1])]
    far = [at for at in offsets if at[0] and at[1]]
    downs, refs = dict(zip(near, refs[: len(near)])), refs[len(near) :]
    down, out, dmat = refs[:3]
    refs = refs[3:]
    (tok, own, core_out, core_in, y_out, y_in, hid, acc, x_out, x_in, z_out, z_in) = refs[:12]
    (s_z, r_z, s_x, r_x, s_c, r_c, s_y, r_y) = refs[12:20]
    s_d, r_d = refs[28:]
    (s_hy, r_hy, s_hc, r_hc, s_bx, r_bx, s_bz, r_bz) = refs[20:28]
    rows, width = out.shape
    h = down.shape[0]
    ctx, tp = lax.axis_index("ctx"), lax.axis_index("tp")
    z, x, y, c = ctx // nx, ctx % nx, tp // nc, tp % nc

    def ctx_at(dz, dx):
        return ((z + dz + nz) % nz * nx + (x + dx + nx) % nx, tp)

    def tp_at(dy, dc):
        return (ctx, (y + dy + ny) % ny * nc + (c + dc + nc) % nc)

    def push(src, dst, send, recv, where):
        copy = pltpu.make_async_remote_copy(
            src_ref=src,
            dst_ref=dst,
            send_sem=send,
            recv_sem=recv,
            device_id=where,
            device_id_type=pl.DeviceIdType.MESH,
        )
        copy.start()
        return copy

    peers = [ctx_at(0, dx) for dx in range(1, nx)]
    if nz > 1:
        peers.append(ctx_at(1, 0))
    if nz > 2:
        peers.append(ctx_at(-1, 0))
    peers += [tp_at(*at) for at in offsets[1:]]
    barrier = pltpu.get_barrier_semaphore()
    for peer in peers:
        pl.semaphore_signal(
            barrier, inc=1, device_id=peer, device_id_type=pl.DeviceIdType.MESH
        )
    pl.semaphore_wait(barrier, len(peers))

    sent = []
    zc, xc, cc, yc, hyc, hcc, bxc, bzc = ({} for _ in range(8))

    def pass_on(dz):
        block = packet if dz == 0 else tok.at[dz, pl.ds(0, rows)]
        if dz:
            zc[dz].wait_recv()
        if dz + 1 < nz:
            zc[dz + 1] = push(
                block, tok.at[dz + 1, pl.ds(0, rows)], s_z.at[dz], r_z.at[dz], ctx_at(1, 0)
            )
            sent.append(zc[dz + 1])
        for dx in range(1, nx):
            xc[dz, dx] = push(
                block,
                tok.at[dz, pl.ds(dx * rows, rows)],
                s_x.at[dz, dx - 1],
                r_x.at[dz, dx - 1],
                ctx_at(0, dx),
            )
            sent.append(xc[dz, dx])

    pass_on(0)
    tok[0, pl.ds(0, rows), :] = packet[...]

    def products(dz):
        for dx in range(1, nx):
            xc[dz, dx].wait_recv()
        for dc in range(nc - 1, -1, -1):
            for dy in range(ny):
                k = dc * ny + dy
                for part, weight in enumerate((gates[k], ups[k])):
                    value = jnp.dot(
                        tok[dz, :, pl.ds(0, width)],
                        weight[...],
                        preferred_element_type=jnp.float32,
                    )
                    if dc:
                        lanes = pl.ds((2 * dy + part) * h, h)
                        core_out[dz, dc - 1, :, lanes] = value.astype(jnp.bfloat16)
                    else:
                        own[dz, dy, :, pl.ds(part * h, h)] = value
            if dc:
                cc[dz, dc] = push(
                    core_out.at[dz, dc - 1],
                    core_in.at[dz, dc - 1],
                    s_c.at[dz, dc - 1],
                    r_c.at[dz, dc - 1],
                    tp_at(0, -dc),
                )
                sent.append(cc[dz, dc])

    def chip_sums(dz):
        for dc in range(1, nc):
            cc[dz, dc].wait_recv()
        for dy in list(range(1, ny)) + [0]:
            value = own[dz, dy]
            for dc in range(1, nc):
                value = value + core_in[dz, dc - 1, :, pl.ds(2 * dy * h, 2 * h)].astype(jnp.float32)
            if dy:
                y_out[dz, dy - 1] = value.astype(jnp.bfloat16)
                yc[dz, dy] = push(
                    y_out.at[dz, dy - 1],
                    y_in.at[dz, dy - 1],
                    s_y.at[dz, dy - 1],
                    r_y.at[dz, dy - 1],
                    tp_at(-dy, 0),
                )
                sent.append(yc[dz, dy])
            else:
                own[dz, 0] = value

    far_copies = []

    def send_down():
        for i, at in enumerate(far):
            begin = pl.multiple_of(tp_at(*at)[1] * width, 128)
            downs[at] = dmat.at[i]
            far_copies.append(
                push(down.at[:, pl.ds(begin, width)], dmat.at[i], s_d.at[i], r_d.at[i], tp_at(*at))
            )
            sent.append(far_copies[-1])

    def activate(dz):
        value = own[dz, 0]
        for dy in range(1, ny):
            yc[dz, dy].wait_recv()
            value = value + y_in[dz, dy - 1].astype(jnp.float32)
        gate, up = value[:, :h], value[:, h:]
        hid[dz, :, pl.ds(0, h)] = (gate / (1.0 + jnp.exp(-gate)) * up).astype(jnp.bfloat16)
        for dy in range(1, ny):
            hyc[dz, dy] = push(
                hid.at[dz, :, pl.ds(0, h)],
                hid.at[dz, :, pl.ds(dy * h, h)],
                s_hy.at[dz, dy - 1],
                r_hy.at[dz, dy - 1],
                tp_at(dy, 0),
            )
            sent.append(hyc[dz, dy])

    def share_hidden(dz):
        for dy in range(1, ny):
            hyc[dz, dy].wait_recv()
        for dc in range(1, nc):
            hcc[dz, dc] = push(
                hid.at[dz, :, pl.ds(0, ny * h)],
                hid.at[dz, :, pl.ds(dc * ny * h, ny * h)],
                s_hc.at[dz, dc - 1],
                r_hc.at[dz, dc - 1],
                tp_at(0, dc),
            )
            sent.append(hcc[dz, dc])

    step = 256 if width % 256 == 0 else 128

    def outputs(dz):
        if dz == 0:
            for copy in far_copies:
                copy.wait_recv()
        for dc in range(1, nc):
            hcc[dz, dc].wait_recv()
        meta = tok[dz, :, pl.ds(width, META)].astype(jnp.float32)
        lane = lax.broadcasted_iota(jnp.int32, meta.shape, 1)
        picked = (lane == ctx) | (lane == ctx + META // 2)
        gate = jnp.sum(jnp.where(picked, meta, 0.0), axis=1, keepdims=True)
        for j in range(width // step):
            cols = pl.ds(j * step, step)
            value = jnp.zeros((nx * rows, step), jnp.float32)
            for k, at in enumerate(offsets):
                value = value + jnp.dot(
                    hid[dz, :, pl.ds(k * h, h)],
                    downs[at][:, cols],
                    preferred_element_type=jnp.float32,
                )
            value = value * gate
            acc[dz, :, cols] = value[:rows]
            for dx in range(1, nx):
                x_out[dz, dx - 1, :, cols] = value[dx * rows : (dx + 1) * rows].astype(jnp.bfloat16)
        for dx in range(1, nx):
            bxc[dz, dx] = push(
                x_out.at[dz, dx - 1],
                x_in.at[dz, dx - 1],
                s_bx.at[dz, dx - 1],
                r_bx.at[dz, dx - 1],
                ctx_at(0, -dx),
            )
            sent.append(bxc[dz, dx])

    def give_back(dz):
        value = acc[dz]
        for dx in range(1, nx):
            bxc[dz, dx].wait_recv()
            value = value + x_in[dz, dx - 1].astype(jnp.float32)
        if dz != 1 and nz > 1:
            before = (dz or nz) - 1
            bzc[before].wait_recv()
            value = value + z_in[before - 1].astype(jnp.float32)
        if dz:
            z_out[dz - 1] = value.astype(jnp.bfloat16)
            bzc[dz] = push(
                z_out.at[dz - 1], z_in.at[dz - 1], s_bz.at[dz - 1], r_bz.at[dz - 1], ctx_at(1, 0)
            )
            sent.append(bzc[dz])
        else:
            out[...] = value

    for turn in range(nz + 3):
        if turn + 1 < nz:
            pass_on(turn + 1)
        if turn < nz:
            products(turn)
        if 0 <= turn - 1 < nz:
            chip_sums(turn - 1)
        if turn == 1:
            send_down()
        if 0 <= turn - 2 < nz:
            share_hidden(turn - 2)
        if 0 <= turn - 1 < nz:
            activate(turn - 1)
        if 0 <= turn - 2 < nz:
            outputs(turn - 2)
        if 1 <= turn - 3 < nz:
            give_back(turn - 3)
    give_back(0)
    for copy in sent:
        copy.wait_send()


def expert_call(dims, packet, gates, ups, downs, down):
    nz, nx, ny, nc = dims
    n_tp = ny * nc
    rows = packet.shape[0]
    width = packet.shape[1] - META
    h = down.shape[0]
    n_far = max(n_tp - len(downs), 1)
    all_rows = nx * rows
    px, py, pc, pz = max(nx - 1, 1), max(ny - 1, 1), max(nc - 1, 1), max(nz - 1, 1)
    bf16, f32 = jnp.bfloat16, jnp.float32
    vmem = pl.BlockSpec(memory_space=pltpu.VMEM)
    sem = pltpu.SemaphoreType.DMA
    shapes = [
        pltpu.VMEM((n_far, h, width), bf16),
        pltpu.VMEM((nz, all_rows, width + META), bf16),
        pltpu.VMEM((nz, ny, all_rows, 2 * h), f32),
        pltpu.VMEM((nz, pc, all_rows, ny * 2 * h), bf16),
        pltpu.VMEM((nz, pc, all_rows, ny * 2 * h), bf16),
        pltpu.VMEM((nz, py, all_rows, 2 * h), bf16),
        pltpu.VMEM((nz, py, all_rows, 2 * h), bf16),
        pltpu.VMEM((nz, all_rows, n_tp * h), bf16),
        pltpu.VMEM((nz, rows, width), f32),
        pltpu.VMEM((nz, px, rows, width), bf16),
        pltpu.VMEM((nz, px, rows, width), bf16),
        pltpu.VMEM((pz, rows, width), bf16),
        pltpu.VMEM((pz, rows, width), bf16),
    ]
    sems = []
    for shape in ((pz,), (nz, px), (nz, pc), (nz, py), (nz, py), (nz, pc), (nz, px), (pz,), (n_far,)):
        sems += [sem(shape), sem(shape)]
    flops = 2 * nz * all_rows * width * n_tp * h * 3
    return pl.pallas_call(
        functools.partial(expert_kernel, dims),
        out_shape=jax.ShapeDtypeStruct((rows, width), f32),
        in_specs=[vmem] * (1 + 2 * n_tp + len(downs)) + [pl.BlockSpec(memory_space=pl.ANY)],
        out_specs=vmem,
        scratch_shapes=shapes + sems,
        compiler_params=pltpu.CompilerParams(
            collective_id=1, has_side_effects=True, vmem_limit_bytes=58 * 1024 * 1024
        ),
        cost_estimate=pl.CostEstimate(
            flops=flops, bytes_accessed=16 * 1024 * 1024, transcendentals=0
        ),
        name="experts",
    )(packet, *gates, *ups, *downs, down)


def solution(mesh):
    return jax.shard_map(
        body,
        mesh=mesh,
        in_specs=(
            P("ctx", "tp"),
            P("ctx", "tp"),
            P("ctx", "tp"),
            P(None, "ctx"),
            P(None, "ctx"),
            P("tp", None, None),
            P("tp", None, None),
            P("tp", None),
            P(),
            P(),
            P("ctx", None),
            P("ctx", None, "tp"),
            P("ctx", None, "tp"),
            P("ctx", "tp", None),
        ),
        out_specs=P("ctx", "tp"),
        check_vma=False,
    )
```
